512 devices in a mesh: rep: 16 (over y, core), shard: 32 (over x, z).
Axes of the slice: x: 4, y: 8, z: 8, core: 2. Of those that a mesh axis runs over, the one named last changes fastest.
Arguments:
- weights: bfloat16 [16, 4096, 5120], P('rep', 'shard'), may hold values from -12 to 12
- warm_start: bfloat16 [16, 2, 16, 5120], P('rep'), may hold values from -4 to 4, as said below
Outputs:
- corrected: bfloat16 [16, 4096, 5120], P('rep', 'shard')
- factors: float32 [16, 2, 16, 5120], P('rep')
The draws below stay inside these ranges and needn't reach their ends.
Inputs may be any that keep to these rules, and one draw needn't show every extreme that they name: `warm_start`: replicas whose indices differ only in bit 0 hold equal start vectors for matching 0, and replicas whose indices differ by 8 hold equal start vectors for matching 1.
All inputs are finite; a program needn't handle non-finite values.
Results may differ from the reference program's by a relative error of at most 0.0049.
Values sent between devices are 32-bit elements; how exact they have to be, the bound alone decides.
No kernel may reach another device: no remote copies, remote signals or barrier semaphores. Data moves between devices by JAX's collectives and lax.ppermute only.
A program may use at most 64 MiB of HBM per device.

```python
import jax
import jax.numpy as jnp
import numpy as np
from jax import lax

ROWS = 4096
COLS = 5120
RANK = 16
STEPS = 2
REP = 16
HALF_REP = 8


def draw_weights(key, part):
    noise_key, scale_key = jax.random.split(jax.random.fold_in(key, 11))
    values = jnp.clip(jax.random.normal(noise_key, (REP, ROWS, COLS), jnp.float32), -4.0, 4.0)
    position = jnp.arange(ROWS).astype(jnp.float32) / ROWS
    roughness = jnp.exp(jax.random.uniform(scale_key, (REP, ROWS, 1), jnp.float32, 0.0, 1.2))
    row_scale = 0.3 * jnp.exp(jnp.log(3.0) * position)[None, :, None] * roughness
    return (values * row_scale).astype(jnp.bfloat16)


def draw_warm_start(key, part):
    noise_key = jax.random.fold_in(key, 23)
    values = jnp.clip(jax.random.normal(noise_key, (REP, STEPS, RANK, COLS), jnp.float32), -4.0, 4.0)
    replica = jnp.arange(REP)
    first_pair = replica - replica % 2
    second_pair = replica % HALF_REP
    return jnp.stack([values[first_pair, 0], values[second_pair, 1]], axis=1).astype(jnp.bfloat16)


def setup_inputs(seed: int = 0) -> dict:
    seeds = jax.random.split(jax.random.key(seed), 3)
    return {
        "weights": draw_weights(jax.random.fold_in(seeds[2], 71), 0),
        "warm_start": draw_warm_start(jax.random.fold_in(seeds[2], 71), 0),
    }


def partner_table(matching):
    replica = np.arange(REP)
    if matching == 0:
        return (replica ^ 1, 1.0 - 2.0 * (replica % 2))
    return (replica ^ HALF_REP, 1.0 - 2.0 * (replica // HALF_REP))

def project_rows(operands):
    return lax.dot_general(operands[0].astype(jnp.float32), operands[1].astype(jnp.float32), (((1,), (1,)), ((), ())), preferred_element_type=jnp.float32)

def project_back(operands):
    return jnp.dot(operands[0].astype(jnp.float32), operands[1].astype(jnp.float32), preferred_element_type=jnp.float32)

def apply_update(operands):
    weight_block, basis_rows, factor_rows, sign_value = operands
    change = lax.dot_general(basis_rows, factor_rows, (((0,), (0,)), ((), ())), precision=lax.Precision.HIGHEST)
    return (weight_block.astype(jnp.float32) - 0.5 * sign_value * change).astype(jnp.bfloat16)

def reference(weights, warm_start):
    current = weights
    factor_list = []
    for matching in range(STEPS):
        partner, parity = partner_table(matching)
        sign_values = jnp.asarray(parity, jnp.float32)
        sign_column = sign_values[:, None, None]
        starts = warm_start[:, matching]
        sketch = lax.map(project_rows, (starts, current))
        differ = sign_column * (sketch - sketch[partner])
        gram_sum = jnp.einsum('rkn,rln->rkl', differ, differ, precision=lax.Precision.HIGHEST)
        triangle = jnp.linalg.cholesky(gram_sum)
        basis_rows = lax.linalg.triangular_solve(triangle, differ, left_side=True, lower=True)
        basis_half = basis_rows.astype(jnp.bfloat16)
        signed = sign_column * lax.map(project_back, (basis_half, current))
        factors = signed + signed[partner]
        current = lax.map(apply_update, (current, basis_rows, factors, sign_values))
        factor_list.append(factors)
    return (current, jnp.stack(factor_list, axis=1))
```

```python
import functools

import jax
import jax.numpy as jnp
from jax import lax
from jax.experimental import pallas as pl
from jax.experimental.pallas import tpu as pltpu
from jax.sharding import Mesh
from jax.sharding import PartitionSpec as P

RANK = 16
LANES = 128
NX, NZ = 4, 8
TILES = 10
GROUP = 32
HIGHEST = lax.Precision.HIGHEST
F32 = jnp.float32
BF16 = jnp.bfloat16
VMEM = pl.BlockSpec(memory_space=pltpu.VMEM)


def call(body, out, ins, flops=1_000_000, data=1_000_000):
    return pl.pallas_call(
        body,
        out_shape=out,
        in_specs=[VMEM] * ins,
        out_specs=jax.tree.map(lambda _: VMEM, out),
        compiler_params=pltpu.CompilerParams(vmem_limit_bytes=40 * 2**20),
        cost_estimate=pl.CostEstimate(flops=flops, bytes_accessed=data, transcendentals=0),
    )


def shape(*dims, dtype=F32):
    return jax.ShapeDtypeStruct(dims, dtype)


def dot(a, b, precision=HIGHEST):
    return jnp.dot(a, b, precision=precision, preferred_element_type=F32)


def dot_t(a, b, precision=HIGHEST):
    return lax.dot_general(
        a, b, (((1,), (1,)), ((), ())), precision=precision, preferred_element_type=F32
    )


def pieces(value):
    high = value.astype(BF16)
    return high, (value - high.astype(F32)).astype(BF16)


def signs():
    even = (1 - 2 * lax.axis_index("c")).astype(F32)
    low = (1 - 2 * lax.axis_index("h")).astype(F32)
    return even, low


def sketch_body(sketch_ref, starts_ref, weight_ref, send_ref):
    crossed = lax.dot_general(
        starts_ref[...].astype(BF16),
        weight_ref[...],
        (((1,), (1,)), ((), ())),
        preferred_element_type=F32,
    )
    for n in range(4):
        send_ref[n, 0:32, :] = sketch_ref[...]
        send_ref[n, 32:48, :] = crossed


def project_body(sketch_ref, weight_ref, send_ref, stack_ref):
    half, core = lax.axis_index("h"), lax.axis_index("c")
    even, low = signs()
    mine = sketch_ref[2 * half + core]
    side = sketch_ref[2 * half + 1 - core]
    far = sketch_ref[2 * (1 - half) + core]
    far_side = sketch_ref[2 * (1 - half) + 1 - core]
    cross = low * (mine[16:32] - far[16:32])
    own = even * (mine[0:16] - side[0:16])
    other = even * (far[0:16] - far_side[0:16])
    start_own = even * (mine[16:32] - side[32:48])
    start_other = even * (far[16:32] - far_side[32:48])
    stack = jnp.concatenate([cross, own, other], axis=0)
    stack_ref[...] = stack
    zero = jnp.zeros((RANK, LANES), F32)

    def gram_rows(left, right):
        return dot_t(left, jnp.concatenate(right, axis=0))

    gram = (
        gram_rows(cross, [cross, own, other] + [zero] * 5)
        + gram_rows(own, [zero] * 3 + [own, other, start_own] + [zero] * 2)
        + gram_rows(other, [zero] * 6 + [other, start_other])
    )
    high, low_part = pieces(stack)
    both = jnp.concatenate([high, low_part], axis=0)
    for x in range(NX):
        span = TILES * LANES
        product = jnp.dot(
            both, weight_ref[:, x * span : (x + 1) * span], preferred_element_type=F32
        )
        product = product[0:48] + product[48:96]
        for t in range(TILES):
            send_ref[x, t * 48 : (t + 1) * 48, :] = product[:, t * LANES : (t + 1) * LANES]
        send_ref[x, TILES * 48 : TILES * 48 + 16, :] = gram


def lane_group():
    return lax.broadcasted_iota(jnp.int32, (RANK, LANES), 1) // GROUP


def first_sum_body(got_ref, send_ref):
    def total(start, size):
        rows = pl.ds(start, size)
        return (got_ref[0, rows, :] + got_ref[1, rows, :]) + (
            got_ref[2, rows, :] + got_ref[3, rows, :]
        )

    gram = total(TILES * 48, 16)
    lanes = lane_group()
    rests = [total((NZ + k) * 48, 48) for k in range(2)]
    for z in range(NZ):
        send_ref[z, 0:48, :] = total(z * 48, 48)
        k, g = z // 4, z % 4
        packed = jnp.zeros((RANK, LANES), F32)
        for a in range(3):
            piece = rests[k][16 * a : 16 * a + 16]
            shift = (GROUP * (a - g)) % LANES
            if shift:
                piece = pltpu.roll(piece, shift, 1)
            packed = jnp.where(lanes == a, piece, packed)
        send_ref[z, 48:64, :] = packed
        send_ref[z, 64:80, :] = gram


def second_sum_body(got_ref, sums_ref, side_ref, gram_ref):
    total = got_ref[0]
    for z in range(1, NZ):
        total = total + got_ref[z]
    sums_ref[...] = total[0:64]
    side_ref[0:16, :] = total[16:32]
    side_ref[16:32, :] = total[48:64]
    gram_ref[...] = total[64:80]


def eye():
    rows = lax.broadcasted_iota(jnp.int32, (RANK, RANK), 0)
    cols = lax.broadcasted_iota(jnp.int32, (RANK, RANK), 1)
    return rows, (rows == cols).astype(F32)


def inverse_factors(grams):
    rows, unit = eye()
    left = list(grams)
    right = [unit] * len(grams)
    for j in range(RANK - 1):
        for i in range(len(grams)):
            ratio = left[i][:, j : j + 1] / left[i][j : j + 1, j : j + 1]
            ratio = jnp.where(rows > j, ratio, 0.0)
            left[i] = left[i] - ratio * left[i][j : j + 1, :]
            right[i] = right[i] - ratio * right[i][j : j + 1, :]
    out = []
    for i in range(len(grams)):
        pivots = jnp.sum(left[i] * unit, axis=1, keepdims=True)
        out.append(right[i] * lax.rsqrt(pivots))
    return out


def factor_body(gram_ref, stack_ref, mix_ref, basis_ref):
    even, low = signs()
    scale = -0.5 * low * even
    blocks = [gram_ref[:, 16 * b : 16 * b + 16] for b in range(8)]
    b0, b1, b2, b3, b4, b5, b6, b7 = blocks
    inv_own, inv_other = inverse_factors([b3, b6])
    gamma_own = dot(inv_own.T, inv_own)
    gamma_other = dot(inv_other.T, inv_other)
    q_own, q_other = b5.T, b7.T
    m_own = scale * dot(q_own, gamma_own)
    m_other = -scale * dot(q_other, gamma_other)
    kg0 = b0 + dot_t(m_own, b1) + dot_t(m_other, b2)
    kg1 = b1 + scale * q_own + dot_t(m_other, b4)
    kg2 = b2 + dot(m_own, b4) - scale * q_other
    gram1 = kg0 + dot_t(kg1, m_own) + dot_t(kg2, m_other)
    (inv1,) = inverse_factors([gram1])
    c_own = scale * even * dot(inv1, dot(kg1, gamma_own))
    c_other = -scale * even * dot(inv1, dot(kg2, gamma_other))
    n_own = dot(inv1, m_own)
    n_other = dot(inv1, m_other)
    zero = jnp.zeros((RANK, RANK), F32)
    first = [zero, even * inv_own, zero, -even * inv_own, zero, zero, zero, zero]
    second = [
        low * inv1,
        low * n_own + c_own,
        low * n_other,
        -c_own,
        -low * inv1,
        c_other - low * n_other,
        -low * n_own,
        -c_other,
    ]
    for b in range(8):
        mix_ref[0:16, 16 * b : 16 * b + 16] = first[b]
        mix_ref[16:32, 16 * b : 16 * b + 16] = second[b]
    cross, own, other = stack_ref[0:16], stack_ref[16:32], stack_ref[32:48]
    basis0 = (0.5 * even) * dot(inv_own, own)
    basis1 = (0.5 * low) * (dot(inv1, cross) + dot(n_own, own) + dot(n_other, other))
    basis_ref[...] = jnp.concatenate([basis0, basis1], axis=0)


def combine_body(sums_ref, side_ref, far_ref, far_side_ref, mix_ref, send_ref):
    rest, far_rest = sums_ref[48:64], far_ref[48:64]
    side_rest, far_side_rest = side_ref[16:32], far_side_ref[16:32]

    def turned(value, a):
        return pltpu.roll(value, LANES - GROUP * a, 1) if a else value

    main = jnp.concatenate(
        [sums_ref[0:48], side_ref[0:16], far_ref[0:48], far_side_ref[0:16]], axis=0
    )
    tail = jnp.concatenate(
        [turned(rest, a) for a in range(3)]
        + [turned(side_rest, 1)]
        + [turned(far_rest, a) for a in range(3)]
        + [turned(far_side_rest, 1)],
        axis=0,
    )
    mix = mix_ref[...]
    head = dot(mix, main)
    tail = dot(mix, tail)
    lanes = lane_group()[0:8]
    packed = tail[0:8]
    for a in range(1, 4):
        packed = jnp.where(lanes == a, pltpu.roll(tail[8 * a : 8 * a + 8], GROUP * a, 1), packed)
    for n in range(NX * NZ):
        send_ref[n, 0:32, :] = head
        send_ref[n, 32:40, :] = packed


def update_body(got_ref, weight_ref, basis_ref, corrected_ref, factors_ref):
    lanes = lane_group()[0:8]
    tiles = [got_ref[z, 0:32, :] for z in range(NZ)]
    for k in range(2):
        groups = []
        for a in range(4):
            row = None
            for g in range(4):
                piece = got_ref[4 * k + g, 32:40, :]
                shift = (GROUP * (g - a)) % LANES
                if shift:
                    piece = pltpu.roll(piece, shift, 1)
                row = piece if row is None else jnp.where(lanes == g, piece, row)
            groups.append(row)
        tiles.append(jnp.concatenate(groups, axis=0))
    transposed = basis_ref[...].T
    columns = []
    for k in range(2):
        high, low = pieces(transposed[:, 16 * k : 16 * k + 16])
        columns.append(jnp.concatenate([high, low, high], axis=1))
    for t in range(TILES):
        span = pl.ds(t * LANES, LANES)
        current = weight_ref[:, span].astype(F32)
        for k in range(2):
            factor = tiles[t][16 * k : 16 * k + 16]
            factors_ref[0, k, :, span] = factor
            high, low = pieces(factor)
            change = jnp.dot(
                columns[k], jnp.concatenate([high, high, low], axis=0), preferred_element_type=F32
            )
            rounded = (current - change).astype(BF16)
            current = rounded.astype(F32)
        corrected_ref[:, span] = rounded


def flip(value, axis):
    return lax.ppermute(value, axis, [(0, 1), (1, 0)])


def flip_both(value):
    return lax.ppermute(value, ("h", "c"), [(0, 3), (1, 2), (2, 1), (3, 0)])


def shards(weights, warm_start):
    weight = weights[0]
    starts = warm_start[0]
    rows, cols = weight.shape
    swapped = flip(starts[1].astype(F32), "c")
    sketch = lax.dot_general(
        starts.reshape(2 * RANK, cols),
        weight,
        (((1,), (1,)), ((), ())),
        preferred_element_type=F32,
    )
    sketch = call(sketch_body, shape(4, 48, rows), 3)(sketch, swapped, weight)
    sketch = lax.all_to_all(sketch, ("h", "c"), 0, 0)
    depth = TILES * 48 + 16
    send, stack = call(
        project_body, (shape(NX, depth, LANES), shape(48, LANES)), 2, 130_000_000, 4_000_000
    )(sketch, weight)
    got = lax.all_to_all(send, "x", 0, 0)
    send = call(first_sum_body, shape(NZ, 80, LANES), 1)(got)
    got = lax.all_to_all(send, "z", 0, 0)
    sums, side, gram = call(
        second_sum_body, (shape(64, LANES), shape(32, LANES), shape(16, LANES)), 1
    )(got)
    far = flip(sums, "h")
    near_side = flip(side, "c")
    far_side = flip_both(side)
    mix, basis = call(
        factor_body, (shape(32, LANES), shape(32, LANES)), 2, 500_000_000, 10_000_000
    )(gram, stack)
    send = call(combine_body, shape(NX * NZ, 40, LANES), 5)(sums, near_side, far, far_side, mix)
    got = lax.all_to_all(send, ("x", "z"), 0, 0)
    span = TILES * LANES
    corrected, factors = pl.pallas_call(
        update_body,
        grid=(NX,),
        out_shape=(shape(rows, cols, dtype=BF16), shape(1, 2, RANK, cols)),
        in_specs=[
            pl.BlockSpec((NZ, 40, LANES), lambda i: (i, 0, 0)),
            pl.BlockSpec((rows, span), lambda i: (0, i)),
            pl.BlockSpec((32, LANES), lambda i: (0, 0)),
        ],
        out_specs=(
            pl.BlockSpec((rows, span), lambda i: (0, i)),
            pl.BlockSpec((1, 2, RANK, span), lambda i: (0, 0, 0, i)),
        ),
        compiler_params=pltpu.CompilerParams(vmem_limit_bytes=40 * 2**20),
    )(got, weight, basis)
    return corrected[None], factors


def solution(mesh):
    inner = Mesh(mesh.devices.reshape(2, 4, 2, NX, NZ), ("h", "y", "c", "x", "z"))
    placed = (P(("h", "y", "c"), ("x", "z"), None), P(("h", "y", "c"), None, None, None))
    return jax.shard_map(
        shards, mesh=inner, in_specs=placed, out_specs=placed, check_vma=False
    )
```

```python
import functools

import jax
import jax.numpy as jnp
from jax import lax
from jax.experimental import pallas as pl
from jax.experimental.pallas import tpu as pltpu
from jax.sharding import Mesh
from jax.sharding import PartitionSpec as P

RANK = 16
LANES = 128
NX, NZ = 4, 8
TILES = 10
GROUP = 32
HIGHEST = lax.Precision.HIGHEST
F32 = jnp.float32
BF16 = jnp.bfloat16
VMEM = pl.BlockSpec(memory_space=pltpu.VMEM)


def call(body, out, ins, flops=1_000_000, data=1_000_000):
    return pl.pallas_call(
        body,
        out_shape=out,
        in_specs=[VMEM] * ins,
        out_specs=jax.tree.map(lambda _: VMEM, out),
        compiler_params=pltpu.CompilerParams(vmem_limit_bytes=40 * 2**20),
        cost_estimate=pl.CostEstimate(flops=flops, bytes_accessed=data, transcendentals=0),
    )


def shape(*dims, dtype=F32):
    return jax.ShapeDtypeStruct(dims, dtype)


def dot(a, b, precision=HIGHEST):
    return jnp.dot(a, b, precision=precision, preferred_element_type=F32)


def dot_t(a, b, precision=HIGHEST):
    return lax.dot_general(
        a, b, (((1,), (1,)), ((), ())), precision=precision, preferred_element_type=F32
    )


def pieces(value):
    high = value.astype(BF16)
    return high, (value - high.astype(F32)).astype(BF16)


def signs():
    even = (1 - 2 * lax.axis_index("c")).astype(F32)
    low = (1 - 2 * lax.axis_index("h")).astype(F32)
    return even, low


def sketch_body(sketch_ref, starts_ref, weight_ref, send_ref):
    crossed = lax.dot_general(
        starts_ref[...].astype(BF16),
        weight_ref[...],
        (((1,), (1,)), ((), ())),
        preferred_element_type=F32,
    )
    for n in range(4):
        send_ref[n, 0:32, :] = sketch_ref[...]
        send_ref[n, 32:48, :] = crossed


def project_body(sketch_ref, weight_ref, send_ref, stack_ref):
    half, core = lax.axis_index("h"), lax.axis_index("c")
    even, low = signs()
    mine = sketch_ref[2 * half + core]
    side = sketch_ref[2 * half + 1 - core]
    far = sketch_ref[2 * (1 - half) + core]
    far_side = sketch_ref[2 * (1 - half) + 1 - core]
    cross = low * (mine[16:32] - far[16:32])
    own = even * (mine[0:16] - side[0:16])
    other = even * (far[0:16] - far_side[0:16])
    start_own = even * (mine[16:32] - side[32:48])
    start_other = even * (far[16:32] - far_side[32:48])
    stack = jnp.concatenate([cross, own, other], axis=0)
    stack_ref[...] = stack
    zero = jnp.zeros((RANK, LANES), F32)

    def gram_rows(left, right):
        return dot_t(left, jnp.concatenate(right, axis=0))

    gram = (
        gram_rows(cross, [cross, own, other] + [zero] * 5)
        + gram_rows(own, [zero] * 3 + [own, other, start_own] + [zero] * 2)
        + gram_rows(other, [zero] * 6 + [other, start_other])
    )
    high, low_part = pieces(stack)
    both = jnp.concatenate([high, low_part], axis=0)
    for x in range(NX):
        span = TILES * LANES
        product = jnp.dot(
            both, weight_ref[:, x * span : (x + 1) * span], preferred_element_type=F32
        )
        product = product[0:48] + product[48:96]
        for t in range(TILES):
            send_ref[x, t * 48 : (t + 1) * 48, :] = product[:, t * LANES : (t + 1) * LANES]
        send_ref[x, TILES * 48 : TILES * 48 + 16, :] = gram


def lane_group():
    return lax.broadcasted_iota(jnp.int32, (RANK, LANES), 1) // GROUP


def first_sum_body(got_ref, send_ref):
    def total(start, size):
        rows = pl.ds(start, size)
        return (got_ref[0, rows, :] + got_ref[1, rows, :]) + (
            got_ref[2, rows, :] + got_ref[3, rows, :]
        )

    gram = total(TILES * 48, 16)
    lanes = lane_group()
    rests = [total((NZ + k) * 48, 48) for k in range(2)]
    for z in range(NZ):
        send_ref[z, 0:48, :] = total(z * 48, 48)
        k, g = z // 4, z % 4
        packed = jnp.zeros((RANK, LANES), F32)
        for a in range(3):
            piece = rests[k][16 * a : 16 * a + 16]
            shift = (GROUP * (a - g)) % LANES
            if shift:
                piece = pltpu.roll(piece, shift, 1)
            packed = jnp.where(lanes == a, piece, packed)
        send_ref[z, 48:64, :] = packed
        send_ref[z, 64:80, :] = gram


def second_sum_body(got_ref, send_ref, gram_ref):
    total = got_ref[0]
    for z in range(1, NZ):
        total = total + got_ref[z]
    for n in range(4):
        send_ref[n] = total[0:64]
    gram_ref[...] = total[64:80]


def eye():
    rows = lax.broadcasted_iota(jnp.int32, (RANK, RANK), 0)
    cols = lax.broadcasted_iota(jnp.int32, (RANK, RANK), 1)
    return rows, (rows == cols).astype(F32)


def inverse_factors(grams):
    rows, unit = eye()
    left = list(grams)
    right = [unit] * len(grams)
    for j in range(RANK - 1):
        for i in range(len(grams)):
            ratio = left[i][:, j : j + 1] / left[i][j : j + 1, j : j + 1]
            ratio = jnp.where(rows > j, ratio, 0.0)
            left[i] = left[i] - ratio * left[i][j : j + 1, :]
            right[i] = right[i] - ratio * right[i][j : j + 1, :]
    out = []
    for i in range(len(grams)):
        pivots = jnp.sum(left[i] * unit, axis=1, keepdims=True)
        out.append(right[i] * lax.rsqrt(pivots))
    return out


def factor_body(gram_ref, stack_ref, mix_ref, basis_ref):
    even, low = signs()
    scale = -0.5 * low * even
    blocks = [gram_ref[:, 16 * b : 16 * b + 16] for b in range(8)]
    b0, b1, b2, b3, b4, b5, b6, b7 = blocks
    inv_own, inv_other = inverse_factors([b3, b6])
    gamma_own = dot(inv_own.T, inv_own)
    gamma_other = dot(inv_other.T, inv_other)
    q_own, q_other = b5.T, b7.T
    m_own = scale * dot(q_own, gamma_own)
    m_other = -scale * dot(q_other, gamma_other)
    kg0 = b0 + dot_t(m_own, b1) + dot_t(m_other, b2)
    kg1 = b1 + scale * q_own + dot_t(m_other, b4)
    kg2 = b2 + dot(m_own, b4) - scale * q_other
    gram1 = kg0 + dot_t(kg1, m_own) + dot_t(kg2, m_other)
    (inv1,) = inverse_factors([gram1])
    c_own = scale * even * dot(inv1, dot(kg1, gamma_own))
    c_other = -scale * even * dot(inv1, dot(kg2, gamma_other))
    n_own = dot(inv1, m_own)
    n_other = dot(inv1, m_other)
    zero = jnp.zeros((RANK, RANK), F32)
    first = [zero, even * inv_own, zero, -even * inv_own, zero, zero, zero, zero]
    second = [
        low * inv1,
        low * n_own + c_own,
        low * n_other,
        -c_own,
        -low * inv1,
        c_other - low * n_other,
        -low * n_own,
        -c_other,
    ]
    for b in range(8):
        mix_ref[0:16, 16 * b : 16 * b + 16] = first[b]
        mix_ref[16:32, 16 * b : 16 * b + 16] = second[b]
    cross, own, other = stack_ref[0:16], stack_ref[16:32], stack_ref[32:48]
    basis0 = (0.5 * even) * dot(inv_own, own)
    basis1 = (0.5 * low) * (dot(inv1, cross) + dot(n_own, own) + dot(n_other, other))
    basis_ref[...] = jnp.concatenate([basis0, basis1], axis=0)


def combine_body(sums_ref, mix_ref, send_ref):
    half, core = lax.axis_index("h"), lax.axis_index("c")
    mine, side = 2 * half + core, 2 * half + 1 - core
    far, far_side = 2 * (1 - half) + core, 2 * (1 - half) + 1 - core
    rest, far_rest = sums_ref[mine, 48:64, :], sums_ref[far, 48:64, :]
    side_rest, far_side_rest = sums_ref[side, 48:64, :], sums_ref[far_side, 48:64, :]

    def turned(value, a):
        return pltpu.roll(value, LANES - GROUP * a, 1) if a else value

    main = jnp.concatenate(
        [
            sums_ref[mine, 0:48, :],
            sums_ref[side, 16:32, :],
            sums_ref[far, 0:48, :],
            sums_ref[far_side, 16:32, :],
        ],
        axis=0,
    )
    tail = jnp.concatenate(
        [turned(rest, a) for a in range(3)]
        + [turned(side_rest, 1)]
        + [turned(far_rest, a) for a in range(3)]
        + [turned(far_side_rest, 1)],
        axis=0,
    )
    mix = mix_ref[...]
    head = dot(mix, main)
    tail = dot(mix, tail)
    lanes = lane_group()[0:8]
    packed = tail[0:8]
    for a in range(1, 4):
        packed = jnp.where(lanes == a, pltpu.roll(tail[8 * a : 8 * a + 8], GROUP * a, 1), packed)
    for n in range(NX * NZ):
        send_ref[n, 0:32, :] = head
        send_ref[n, 32:40, :] = packed


def update_body(
    got_ref, weight_ref, basis_ref, corrected_hbm, factors_hbm, corrected_ref, factors_ref, sems
):
    lanes = lane_group()[0:8]
    span = TILES * LANES
    transposed = basis_ref[...].T
    left = []
    for k in range(2):
        high, low = pieces(transposed[:, 16 * k : 16 * k + 16])
        left.append(jnp.concatenate([high, low, high], axis=1))
    copies = []
    for x in range(NX):
        tiles = [got_ref[x * NZ + z, 0:32, :] for z in range(NZ)]
        for k in range(2):
            groups = []
            for a in range(4):
                row = None
                for g in range(4):
                    piece = got_ref[x * NZ + 4 * k + g, 32:40, :]
                    shift = (GROUP * (g - a)) % LANES
                    if shift:
                        piece = pltpu.roll(piece, shift, 1)
                    row = piece if row is None else jnp.where(lanes == g, piece, row)
                groups.append(row)
            tiles.append(jnp.concatenate(groups, axis=0))
        for t in range(0, TILES, 2):
            part = pl.ds(x * span + t * LANES, 2 * LANES)
            pair = jnp.concatenate(tiles[t : t + 2], axis=1)
            current = weight_ref[:, part].astype(F32)
            for k in range(2):
                factor = pair[16 * k : 16 * k + 16]
                factors_ref[k, :, part] = factor
                high, low = pieces(factor)
                right = jnp.concatenate([high, high, low], axis=0)
                change = jnp.dot(left[k], right, preferred_element_type=F32)
                rounded = (current - change).astype(BF16)
                current = rounded.astype(F32)
            corrected_ref[:, part] = rounded
        part = pl.ds(x * span, span)
        for i, (source, target) in enumerate(
            ((corrected_ref, corrected_hbm), (factors_ref, factors_hbm))
        ):
            index = (slice(None),) * (1 + i) + (part,)
            copy = pltpu.make_async_copy(source.at[index], target.at[index], sems.at[2 * x + i])
            copy.start()
            copies.append(copy)
    for copy in copies:
        copy.wait()


def flip(value, axis):
    return lax.ppermute(value, axis, [(0, 1), (1, 0)])


def shards(weights, warm_start):
    weight = weights[0]
    starts = warm_start[0]
    rows, cols = weight.shape
    swapped = flip(starts[1].astype(F32), "c")
    sketch = lax.dot_general(
        starts.reshape(2 * RANK, cols),
        weight,
        (((1,), (1,)), ((), ())),
        preferred_element_type=F32,
    )
    sketch = call(sketch_body, shape(4, 48, rows), 3)(sketch, swapped, weight)
    sketch = lax.all_to_all(sketch, ("h", "c"), 0, 0)
    depth = TILES * 48 + 16
    send, stack = call(
        project_body, (shape(NX, depth, LANES), shape(48, LANES)), 2, 130_000_000, 4_000_000
    )(sketch, weight)
    got = lax.all_to_all(send, "x", 0, 0)
    send = call(first_sum_body, shape(NZ, 80, LANES), 1)(got)
    got = lax.all_to_all(send, "z", 0, 0)
    send, gram = call(second_sum_body, (shape(4, 64, LANES), shape(16, LANES)), 1)(got)
    sums = lax.all_to_all(send, ("h", "c"), 0, 0)
    mix, basis = call(
        factor_body, (shape(32, LANES), shape(32, LANES)), 2, 500_000_000, 10_000_000
    )(gram, stack)
    send = call(combine_body, shape(NX * NZ, 40, LANES), 2)(sums, mix)
    got = lax.all_to_all(send, ("x", "z"), 0, 0)
    hbm = pl.BlockSpec(memory_space=pltpu.HBM)
    corrected, factors = pl.pallas_call(
        update_body,
        out_shape=(shape(rows, cols, dtype=BF16), shape(2, RANK, cols)),
        in_specs=[VMEM] * 3,
        out_specs=(hbm, hbm),
        scratch_shapes=[
            pltpu.VMEM((rows, cols), BF16),
            pltpu.VMEM((2, RANK, cols), F32),
            pltpu.SemaphoreType.DMA((2 * NX,)),
        ],
        compiler_params=pltpu.CompilerParams(vmem_limit_bytes=40 * 2**20),
    )(got, weight, basis)
    return corrected[None], factors[None]


def solution(mesh):
    inner = Mesh(mesh.devices.reshape(2, 4, 2, NX, NZ), ("h", "y", "c", "x", "z"))
    placed = (P(("h", "y", "c"), ("x", "z"), None), P(("h", "y", "c"), None, None, None))
    return jax.shard_map(
        shards, mesh=inner, in_specs=placed, out_specs=placed, check_vma=False
    )
```

```python
import functools

import jax
import jax.numpy as jnp
from jax import lax
from jax.experimental import pallas as pl
from jax.experimental.pallas import tpu as pltpu
from jax.sharding import Mesh
from jax.sharding import PartitionSpec as P

RANK = 16
LANES = 128
FIRST, FIRST_SIZE = ("x", "v"), 8
SECOND, SECOND_SIZE = ("w",), 4
TILES = 40 // FIRST_SIZE
REST = TILES - SECOND_SIZE
OWNERS = FIRST_SIZE * SECOND_SIZE
SPLIT_GATHER = True
GROUP = 32
HIGHEST = lax.Precision.HIGHEST
F32 = jnp.float32
BF16 = jnp.bfloat16
VMEM = pl.BlockSpec(memory_space=pltpu.VMEM)


def call(body, out, ins, flops=1_000_000, data=1_000_000):
    return pl.pallas_call(
        body,
        out_shape=out,
        in_specs=[VMEM] * ins,
        out_specs=jax.tree.map(lambda _: VMEM, out),
        compiler_params=pltpu.CompilerParams(vmem_limit_bytes=40 * 2**20),
        cost_estimate=pl.CostEstimate(flops=flops, bytes_accessed=data, transcendentals=0),
    )


def shape(*dims, dtype=F32):
    return jax.ShapeDtypeStruct(dims, dtype)


def dot(a, b, precision=HIGHEST):
    return jnp.dot(a, b, precision=precision, preferred_element_type=F32)


def dot_t(a, b, precision=HIGHEST):
    return lax.dot_general(
        a, b, (((1,), (1,)), ((), ())), precision=precision, preferred_element_type=F32
    )


def pieces(value):
    high = value.astype(BF16)
    return high, (value - high.astype(F32)).astype(BF16)


def signs():
    even = (1 - 2 * lax.axis_index("c")).astype(F32)
    low = (1 - 2 * lax.axis_index("h")).astype(F32)
    return even, low


def sketch_body(sketch_ref, starts_ref, weight_ref, send_ref):
    send_ref[0:16, :] = sketch_ref[0:16]
    send_ref[16:32, :] = dot_t(starts_ref[...].astype(BF16), weight_ref[...], None)


def differ_body(sketch_ref, mine_ref, side_ref, send_ref):
    even, _ = signs()
    send_ref[0:16, :] = even * (mine_ref[0:16] - side_ref[0:16])
    send_ref[16:32, :] = even * (sketch_ref[16:32] - side_ref[16:32])
    send_ref[32:48, :] = sketch_ref[16:32]


def project_body(mine_ref, far_ref, weight_ref, send_ref, stack_ref):
    _, low = signs()
    own, start_own = mine_ref[0:16], mine_ref[16:32]
    other, start_other = far_ref[0:16], far_ref[16:32]
    cross = low * (mine_ref[32:48] - far_ref[32:48])
    stack = jnp.concatenate([cross, own, other], axis=0)
    stack_ref[...] = stack
    zero = jnp.zeros((RANK, LANES), F32)

    def gram_rows(left, right):
        return dot_t(left, jnp.concatenate(right, axis=0))

    gram = (
        gram_rows(cross, [cross, own, other] + [zero] * 5)
        + gram_rows(own, [zero] * 3 + [own, other, start_own] + [zero] * 2)
        + gram_rows(other, [zero] * 6 + [other, start_other])
    )
    high, low_part = pieces(stack)
    both = jnp.concatenate([high, low_part], axis=0)
    for x in range(FIRST_SIZE):
        span = TILES * LANES
        product = jnp.dot(
            both, weight_ref[:, x * span : (x + 1) * span], preferred_element_type=F32
        )
        product = product[0:48] + product[48:96]
        for t in range(TILES):
            send_ref[x, t * 48 : (t + 1) * 48, :] = product[:, t * LANES : (t + 1) * LANES]
        send_ref[x, TILES * 48 : TILES * 48 + 16, :] = gram


def lane_group():
    return lax.broadcasted_iota(jnp.int32, (RANK, LANES), 1) // GROUP


def added(values):
    while len(values) > 1:
        values = [a + b for a, b in zip(values[::2], values[1::2])]
    return values[0]


def first_sum_body(got_ref, send_ref):
    def total(start, size):
        return added([got_ref[x, start : start + size, :] for x in range(FIRST_SIZE)])

    gram = total(TILES * 48, 16)
    lanes = lane_group()
    rests = [total((SECOND_SIZE + k) * 48, 48) for k in range(REST)]
    for z in range(SECOND_SIZE):
        send_ref[z, 0:48, :] = total(z * 48, 48)
        k, g = z // 4, z % 4
        packed = jnp.zeros((RANK, LANES), F32)
        for a in range(3):
            piece = rests[k][16 * a : 16 * a + 16]
            shift = (GROUP * (a - g)) % LANES
            if shift:
                piece = pltpu.roll(piece, shift, 1)
            packed = jnp.where(lanes == a, piece, packed)
        send_ref[z, 48:64, :] = packed
        send_ref[z, 64:80, :] = gram


def second_sum_body(got_ref, sums_ref, side_ref, gram_ref):
    total = added([got_ref[z] for z in range(SECOND_SIZE)])
    sums_ref[...] = total[0:64]
    side_ref[0:16, :] = total[16:32]
    side_ref[16:32, :] = total[48:64]
    gram_ref[...] = total[64:80]


def join_body(sums_ref, side_ref, gram_in_ref, send_ref, gram_ref):
    moved = pltpu.roll(side_ref[16:32], 2 * GROUP, 1)
    send_ref[0:48, :] = sums_ref[0:48]
    send_ref[48:64, :] = jnp.where(lane_group() == 3, moved, sums_ref[48:64])
    send_ref[64:80, :] = side_ref[0:16]
    gram_ref[...] = gram_in_ref[...]


def eye():
    rows = lax.broadcasted_iota(jnp.int32, (RANK, RANK), 0)
    cols = lax.broadcasted_iota(jnp.int32, (RANK, RANK), 1)
    return rows, (rows == cols).astype(F32)


def inverse_factors(grams):
    rows, unit = eye()
    left = list(grams)
    right = [unit] * len(grams)
    for j in range(RANK - 1):
        for i in range(len(grams)):
            ratio = left[i][:, j : j + 1] / left[i][j : j + 1, j : j + 1]
            ratio = jnp.where(rows > j, ratio, 0.0)
            left[i] = left[i] - ratio * left[i][j : j + 1, :]
            right[i] = right[i] - ratio * right[i][j : j + 1, :]
    out = []
    for i in range(len(grams)):
        pivots = jnp.sum(left[i] * unit, axis=1, keepdims=True)
        out.append(right[i] * lax.rsqrt(pivots))
    return out


def factor_body(gram_ref, stack_ref, mix_ref, basis_ref):
    even, low = signs()
    scale = -0.5 * low * even
    blocks = [gram_ref[:, 16 * b : 16 * b + 16] for b in range(8)]
    b0, b1, b2, b3, b4, b5, b6, b7 = blocks
    inv_own, inv_other = inverse_factors([b3, b6])
    gamma_own = dot(inv_own.T, inv_own)
    gamma_other = dot(inv_other.T, inv_other)
    q_own, q_other = b5.T, b7.T
    m_own = scale * dot(q_own, gamma_own)
    m_other = -scale * dot(q_other, gamma_other)
    kg0 = b0 + dot_t(m_own, b1) + dot_t(m_other, b2)
    kg1 = b1 + scale * q_own + dot_t(m_other, b4)
    kg2 = b2 + dot(m_own, b4) - scale * q_other
    gram1 = kg0 + dot_t(kg1, m_own) + dot_t(kg2, m_other)
    (inv1,) = inverse_factors([gram1])
    c_own = scale * even * dot(inv1, dot(kg1, gamma_own))
    c_other = -scale * even * dot(inv1, dot(kg2, gamma_other))
    n_own = dot(inv1, m_own)
    n_other = dot(inv1, m_other)
    zero = jnp.zeros((RANK, RANK), F32)
    first = [zero, even * inv_own, zero, -even * inv_own, zero, zero, zero, zero]
    second = [
        low * inv1,
        low * n_own + c_own,
        low * n_other,
        -c_own,
        -low * inv1,
        c_other - low * n_other,
        -low * n_own,
        -c_other,
    ]
    for b in range(8):
        mix_ref[0:16, 16 * b : 16 * b + 16] = first[b]
        mix_ref[16:32, 16 * b : 16 * b + 16] = second[b]
    cross, own, other = stack_ref[0:16], stack_ref[16:32], stack_ref[32:48]
    basis0 = (0.5 * even) * dot(inv_own, own)
    basis1 = (0.5 * low) * (dot(inv1, cross) + dot(n_own, own) + dot(n_other, other))
    basis_ref[...] = jnp.concatenate([basis0, basis1], axis=0)


def combine_body(sums_ref, side_ref, far_ref, mix_ref, send_ref):
    rest, far_rest = sums_ref[48:64], far_ref[48:64]

    def turned(value, a):
        return pltpu.roll(value, LANES - GROUP * a, 1) if a else value

    main = jnp.concatenate(
        [sums_ref[0:48], side_ref[0:16], far_ref[0:48], far_ref[64:80]], axis=0
    )
    tail = jnp.concatenate(
        [turned(rest, a) for a in range(3)]
        + [turned(side_ref[16:32], 1)]
        + [turned(far_rest, a) for a in range(4)],
        axis=0,
    )
    mix = mix_ref[...]
    head = dot(mix, main)
    tail = dot(mix, tail)
    lanes = lane_group()[0:8]
    packed = tail[0:8]
    for a in range(1, 4):
        packed = jnp.where(lanes == a, pltpu.roll(tail[8 * a : 8 * a + 8], GROUP * a, 1), packed)
    for n in range(send_ref.shape[0]):
        send_ref[n, 0:32, :] = head
        send_ref[n, 32:40, :] = packed


def spread_body(got_ref, send_ref):
    for n in range(FIRST_SIZE):
        for z in range(SECOND_SIZE):
            send_ref[n, z * 40 : (z + 1) * 40, :] = got_ref[z]


def update_body(
    got_ref, weight_ref, basis_ref, corrected_hbm, factors_hbm, corrected_ref, factors_ref, sems
):
    lanes = lane_group()[0:8]
    chunk = 10
    span = chunk * LANES
    transposed = basis_ref[...].T
    left = []
    for k in range(2):
        high, low = pieces(transposed[:, 16 * k : 16 * k + 16])
        left.append(jnp.concatenate([high, low, high], axis=1))
    copies = []
    for x in range(4):
        tiles = []
        for first in range(x * FIRST_SIZE // 4, (x + 1) * FIRST_SIZE // 4):
            base = first * SECOND_SIZE
            tiles += [got_ref[base + z, 0:32, :] for z in range(SECOND_SIZE)]
            for k in range(REST):
                groups = []
                for a in range(4):
                    row = None
                    for g in range(4):
                        piece = got_ref[base + 4 * k + g, 32:40, :]
                        shift = (GROUP * (g - a)) % LANES
                        if shift:
                            piece = pltpu.roll(piece, shift, 1)
                        row = piece if row is None else jnp.where(lanes == g, piece, row)
                    groups.append(row)
                tiles.append(jnp.concatenate(groups, axis=0))
        for t in range(0, chunk, 2):
            part = pl.ds(x * span + t * LANES, 2 * LANES)
            pair = jnp.concatenate(tiles[t : t + 2], axis=1)
            current = weight_ref[:, part].astype(F32)
            for k in range(2):
                factor = pair[16 * k : 16 * k + 16]
                factors_ref[k, :, part] = factor
                high, low = pieces(factor)
                right = jnp.concatenate([high, high, low], axis=0)
                change = jnp.dot(left[k], right, preferred_element_type=F32)
                rounded = (current - change).astype(BF16)
                current = rounded.astype(F32)
            corrected_ref[:, part] = rounded
        part = pl.ds(x * span, span)
        for i, (source, target) in enumerate(
            ((corrected_ref, corrected_hbm), (factors_ref, factors_hbm))
        ):
            index = (slice(None),) * (1 + i) + (part,)
            copy = pltpu.make_async_copy(source.at[index], target.at[index], sems.at[2 * x + i])
            copy.start()
            copies.append(copy)
    for copy in copies:
        copy.wait()


def flip(value, axis):
    return lax.ppermute(value, axis, [(0, 1), (1, 0)])


def shards(weights, warm_start):
    weight = weights[0]
    starts = warm_start[0]
    rows, cols = weight.shape
    swapped = flip(starts[1].astype(F32), "c")
    sketch = lax.dot_general(
        starts.reshape(2 * RANK, cols),
        weight,
        (((1,), (1,)), ((), ())),
        preferred_element_type=F32,
    )
    mine = call(sketch_body, shape(32, rows), 3)(sketch, swapped, weight)
    mine = call(differ_body, shape(48, rows), 3)(sketch, mine, flip(mine, "c"))
    far = flip(mine, "h")
    depth = TILES * 48 + 16
    send, stack = call(
        project_body, (shape(FIRST_SIZE, depth, LANES), shape(48, LANES)), 3, 130_000_000, 4_000_000
    )(mine, far, weight)
    got = lax.all_to_all(send, FIRST, 0, 0)
    send = call(first_sum_body, shape(SECOND_SIZE, 80, LANES), 1)(got)
    got = lax.all_to_all(send, SECOND, 0, 0)
    sums, side, gram = call(
        second_sum_body, (shape(64, LANES), shape(32, LANES), shape(16, LANES)), 1
    )(got)
    side = flip(side, "c")
    send, gram = call(join_body, (shape(80, LANES), shape(16, LANES)), 3)(sums, side, gram)
    far = flip(send, "h")
    mix, basis = call(
        factor_body, (shape(32, LANES), shape(32, LANES)), 2, 500_000_000, 10_000_000
    )(gram, stack)
    copies = SECOND_SIZE if SPLIT_GATHER else OWNERS
    send = call(combine_body, shape(copies, 40, LANES), 4)(sums, side, far, mix)
    if SPLIT_GATHER:
        got = lax.all_to_all(send, SECOND, 0, 0)
        send = call(spread_body, shape(FIRST_SIZE, SECOND_SIZE * 40, LANES), 1)(got)
        got = lax.all_to_all(send, FIRST, 0, 0).reshape(OWNERS, 40, LANES)
    else:
        got = lax.all_to_all(send, FIRST + SECOND, 0, 0)
    hbm = pl.BlockSpec(memory_space=pltpu.HBM)
    corrected, factors = pl.pallas_call(
        update_body,
        out_shape=(shape(rows, cols, dtype=BF16), shape(2, RANK, cols)),
        in_specs=[VMEM] * 3,
        out_specs=(hbm, hbm),
        scratch_shapes=[
            pltpu.VMEM((rows, cols), BF16),
            pltpu.VMEM((2, RANK, cols), F32),
            pltpu.SemaphoreType.DMA((8,)),
        ],
        compiler_params=pltpu.CompilerParams(vmem_limit_bytes=40 * 2**20),
    )(got, weight, basis)
    return corrected[None], factors[None]


def solution(mesh):
    inner = Mesh(mesh.devices.reshape(2, 4, 2, 4, 4, 2), ("h", "y", "c", "x", "w", "v"))
    placed = (P(("h", "y", "c"), ("x", "w", "v"), None), P(("h", "y", "c"), None, None, None))
    return jax.shard_map(
        shards, mesh=inner, in_specs=placed, out_specs=placed, check_vma=False
    )
```

```python
import functools

import jax
import jax.numpy as jnp
from jax import lax
from jax.experimental import pallas as pl
from jax.experimental.pallas import tpu as pltpu
from jax.sharding import Mesh
from jax.sharding import PartitionSpec as P

RANK = 16
LANES = 128
FIRST, FIRST_SIZE = ("x", "v"), 8
SECOND, SECOND_SIZE = ("w",), 4
TILES = 40 // FIRST_SIZE
REST = TILES - SECOND_SIZE
OWNERS = FIRST_SIZE * SECOND_SIZE
GROUP = 32
HIGHEST = lax.Precision.HIGHEST
F32 = jnp.float32
BF16 = jnp.bfloat16
VMEM = pl.BlockSpec(memory_space=pltpu.VMEM)


def call(body, out, ins, flops=1_000_000, data=1_000_000):
    return pl.pallas_call(
        body,
        out_shape=out,
        in_specs=[VMEM] * ins,
        out_specs=jax.tree.map(lambda _: VMEM, out),
        compiler_params=pltpu.CompilerParams(vmem_limit_bytes=40 * 2**20),
        cost_estimate=pl.CostEstimate(flops=flops, bytes_accessed=data, transcendentals=0),
    )


def shape(*dims, dtype=F32):
    return jax.ShapeDtypeStruct(dims, dtype)


def dot(a, b, precision=HIGHEST):
    return jnp.dot(a, b, precision=precision, preferred_element_type=F32)


def dot_t(a, b, precision=HIGHEST):
    return lax.dot_general(
        a, b, (((1,), (1,)), ((), ())), precision=precision, preferred_element_type=F32
    )


def pieces(value):
    high = value.astype(BF16)
    return high, (value - high.astype(F32)).astype(BF16)


def signs():
    even = (1 - 2 * lax.axis_index("c")).astype(F32)
    low = (1 - 2 * lax.axis_index("h")).astype(F32)
    return even, low


def sketch_body(sketch_ref, starts_ref, weight_ref, send_ref):
    send_ref[0:16, :] = sketch_ref[0:16]
    send_ref[16:32, :] = dot_t(starts_ref[...].astype(BF16), weight_ref[...], None)


def differ_body(sketch_ref, mine_ref, side_ref, send_ref):
    even, _ = signs()
    send_ref[0:16, :] = even * (mine_ref[0:16] - side_ref[0:16])
    send_ref[16:32, :] = even * (sketch_ref[16:32] - side_ref[16:32])
    send_ref[32:48, :] = sketch_ref[16:32]


def project_body(mine_ref, far_ref, weight_ref, send_ref, stack_ref):
    _, low = signs()
    own, start_own = mine_ref[0:16], mine_ref[16:32]
    other, start_other = far_ref[0:16], far_ref[16:32]
    cross = low * (mine_ref[32:48] - far_ref[32:48])
    stack = jnp.concatenate([cross, own, other], axis=0)
    stack_ref[...] = stack
    zero = jnp.zeros((RANK, LANES), F32)

    def gram_rows(left, right):
        return dot_t(left, jnp.concatenate(right, axis=0))

    gram = (
        gram_rows(cross, [cross, own, other] + [zero] * 5)
        + gram_rows(own, [zero] * 3 + [own, other, start_own] + [zero] * 2)
        + gram_rows(other, [zero] * 6 + [other, start_other])
    )
    high, low_part = pieces(stack)
    both = jnp.concatenate([high, low_part], axis=0)
    for x in range(FIRST_SIZE):
        span = TILES * LANES
        product = jnp.dot(
            both, weight_ref[:, x * span : (x + 1) * span], preferred_element_type=F32
        )
        product = product[0:48] + product[48:96]
        for t in range(TILES):
            send_ref[x, t * 48 : (t + 1) * 48, :] = product[:, t * LANES : (t + 1) * LANES]
        send_ref[x, TILES * 48 : TILES * 48 + 16, :] = gram


def lane_group():
    return lax.broadcasted_iota(jnp.int32, (RANK, LANES), 1) // GROUP


def added(values):
    while len(values) > 1:
        values = [a + b for a, b in zip(values[::2], values[1::2])]
    return values[0]


def first_sum_body(got_ref, send_ref):
    def total(start, size):
        return added([got_ref[x, start : start + size, :] for x in range(FIRST_SIZE)])

    gram = total(TILES * 48, 16)
    lanes = lane_group()
    rests = [total((SECOND_SIZE + k) * 48, 48) for k in range(REST)]
    for z in range(SECOND_SIZE):
        send_ref[z, 0:48, :] = total(z * 48, 48)
        k, g = z // 4, z % 4
        packed = jnp.zeros((RANK, LANES), F32)
        for a in range(3):
            piece = rests[k][16 * a : 16 * a + 16]
            shift = (GROUP * (a - g)) % LANES
            if shift:
                piece = pltpu.roll(piece, shift, 1)
            packed = jnp.where(lanes == a, piece, packed)
        send_ref[z, 48:64, :] = packed
        send_ref[z, 64:80, :] = gram


def second_sum_body(got_ref, sums_ref, side_ref, gram_ref):
    total = added([got_ref[z] for z in range(SECOND_SIZE)])
    sums_ref[...] = total[0:64]
    side_ref[0:16, :] = total[16:32]
    side_ref[16:32, :] = total[48:64]
    gram_ref[...] = total[64:80]


def join_body(sums_ref, side_ref, gram_in_ref, send_ref, gram_ref):
    moved = pltpu.roll(side_ref[16:32], 2 * GROUP, 1)
    send_ref[0:48, :] = sums_ref[0:48]
    send_ref[48:64, :] = jnp.where(lane_group() == 3, moved, sums_ref[48:64])
    send_ref[64:80, :] = side_ref[0:16]
    gram_ref[...] = gram_in_ref[...]


def eye():
    rows = lax.broadcasted_iota(jnp.int32, (RANK, RANK), 0)
    cols = lax.broadcasted_iota(jnp.int32, (RANK, RANK), 1)
    return rows, (rows == cols).astype(F32)


def inverse_factors(grams):
    rows, unit = eye()
    left = list(grams)
    right = [unit] * len(grams)
    for j in range(RANK - 1):
        for i in range(len(grams)):
            ratio = left[i][:, j : j + 1] / left[i][j : j + 1, j : j + 1]
            ratio = jnp.where(rows > j, ratio, 0.0)
            left[i] = left[i] - ratio * left[i][j : j + 1, :]
            right[i] = right[i] - ratio * right[i][j : j + 1, :]
    out = []
    for i in range(len(grams)):
        pivots = jnp.sum(left[i] * unit, axis=1, keepdims=True)
        out.append(right[i] * lax.rsqrt(pivots))
    return out


def factor_body(gram_ref, stack_ref, mix_ref, basis_ref):
    even, low = signs()
    scale = -0.5 * low * even
    blocks = [gram_ref[:, 16 * b : 16 * b + 16] for b in range(8)]
    b0, b1, b2, b3, b4, b5, b6, b7 = blocks
    inv_own, inv_other = inverse_factors([b3, b6])
    gamma_own = dot(inv_own.T, inv_own)
    gamma_other = dot(inv_other.T, inv_other)
    q_own, q_other = b5.T, b7.T
    m_own = scale * dot(q_own, gamma_own)
    m_other = -scale * dot(q_other, gamma_other)
    kg0 = b0 + dot_t(m_own, b1) + dot_t(m_other, b2)
    kg1 = b1 + scale * q_own + dot_t(m_other, b4)
    kg2 = b2 + dot(m_own, b4) - scale * q_other
    gram1 = kg0 + dot_t(kg1, m_own) + dot_t(kg2, m_other)
    (inv1,) = inverse_factors([gram1])
    c_own = scale * even * dot(inv1, dot(kg1, gamma_own))
    c_other = -scale * even * dot(inv1, dot(kg2, gamma_other))
    n_own = dot(inv1, m_own)
    n_other = dot(inv1, m_other)
    zero = jnp.zeros((RANK, RANK), F32)
    first = [zero, even * inv_own, zero, -even * inv_own, zero, zero, zero, zero]
    second = [
        low * inv1,
        low * n_own + c_own,
        low * n_other,
        -c_own,
        -low * inv1,
        c_other - low * n_other,
        -low * n_own,
        -c_other,
    ]
    for b in range(8):
        mix_ref[0:16, 16 * b : 16 * b + 16] = first[b]
        mix_ref[16:32, 16 * b : 16 * b + 16] = second[b]
    cross, own, other = stack_ref[0:16], stack_ref[16:32], stack_ref[32:48]
    basis0 = (0.5 * even) * dot(inv_own, own)
    basis1 = (0.5 * low) * (dot(inv1, cross) + dot(n_own, own) + dot(n_other, other))
    basis_ref[...] = jnp.concatenate([basis0, basis1], axis=0)


def combine_body(sums_ref, side_ref, far_ref, mix_ref, send_ref):
    rest, far_rest = sums_ref[48:64], far_ref[48:64]

    def turned(value, a):
        return pltpu.roll(value, LANES - GROUP * a, 1) if a else value

    main = jnp.concatenate(
        [sums_ref[0:48], side_ref[0:16], far_ref[0:48], far_ref[64:80]], axis=0
    )
    tail = jnp.concatenate(
        [turned(rest, a) for a in range(3)]
        + [turned(side_ref[16:32], 1)]
        + [turned(far_rest, a) for a in range(4)],
        axis=0,
    )
    mix = mix_ref[...]
    head = dot(mix, main)
    tail = dot(mix, tail)
    lanes = lane_group()[0:8]
    packed = tail[0:8]
    for a in range(1, 4):
        packed = jnp.where(lanes == a, pltpu.roll(tail[8 * a : 8 * a + 8], GROUP * a, 1), packed)
    for n in range(send_ref.shape[0]):
        send_ref[n, 0:32, :] = head
        send_ref[n, 32:40, :] = packed


def update_body(
    got_ref, weight_ref, basis_ref, corrected_hbm, factors_hbm, corrected_ref, factors_ref, sems
):
    lanes = lane_group()[0:8]
    chunk = 10
    span = chunk * LANES
    transposed = basis_ref[...].T
    left = []
    for k in range(2):
        high, low = pieces(transposed[:, 16 * k : 16 * k + 16])
        left.append(jnp.concatenate([high, low, high], axis=1))
    copies = []
    for x in range(4):
        tiles = []
        for first in range(x * FIRST_SIZE // 4, (x + 1) * FIRST_SIZE // 4):
            base = first * SECOND_SIZE
            tiles += [got_ref[base + z, 0:32, :] for z in range(SECOND_SIZE)]
            for k in range(REST):
                groups = []
                for a in range(4):
                    row = None
                    for g in range(4):
                        piece = got_ref[base + 4 * k + g, 32:40, :]
                        shift = (GROUP * (g - a)) % LANES
                        if shift:
                            piece = pltpu.roll(piece, shift, 1)
                        row = piece if row is None else jnp.where(lanes == g, piece, row)
                    groups.append(row)
                tiles.append(jnp.concatenate(groups, axis=0))
        for t in range(0, chunk, 2):
            part = pl.ds(x * span + t * LANES, 2 * LANES)
            pair = jnp.concatenate(tiles[t : t + 2], axis=1)
            current = weight_ref[:, part].astype(F32)
            for k in range(2):
                factor = pair[16 * k : 16 * k + 16]
                factors_ref[k, :, part] = factor
                high, low = pieces(factor)
                right = jnp.concatenate([high, high, low], axis=0)
                change = jnp.dot(left[k], right, preferred_element_type=F32)
                rounded = (current - change).astype(BF16)
                current = rounded.astype(F32)
            corrected_ref[:, part] = rounded
        part = pl.ds(x * span, span)
        for i, (source, target) in enumerate(
            ((corrected_ref, corrected_hbm), (factors_ref, factors_hbm))
        ):
            index = (slice(None),) * (1 + i) + (part,)
            copy = pltpu.make_async_copy(source.at[index], target.at[index], sems.at[2 * x + i])
            copy.start()
            copies.append(copy)
    for copy in copies:
        copy.wait()


def flip(value, axis):
    return lax.ppermute(value, axis, [(0, 1), (1, 0)])


def shards(weights, warm_start):
    weight = weights[0]
    starts = warm_start[0]
    rows, cols = weight.shape
    swapped = flip(starts[1].astype(F32), "c")
    sketch = lax.dot_general(
        starts.reshape(2 * RANK, cols),
        weight,
        (((1,), (1,)), ((), ())),
        preferred_element_type=F32,
    )
    mine = call(sketch_body, shape(32, rows), 3)(sketch, swapped, weight)
    mine = call(differ_body, shape(48, rows), 3)(sketch, mine, flip(mine, "c"))
    far = flip(mine, "h")
    depth = TILES * 48 + 16
    send, stack = call(
        project_body, (shape(FIRST_SIZE, depth, LANES), shape(48, LANES)), 3, 130_000_000, 4_000_000
    )(mine, far, weight)
    got = lax.all_to_all(send, FIRST, 0, 0)
    send = call(first_sum_body, shape(SECOND_SIZE, 80, LANES), 1)(got)
    got = lax.all_to_all(send, SECOND, 0, 0)
    sums, side, gram = call(
        second_sum_body, (shape(64, LANES), shape(32, LANES), shape(16, LANES)), 1
    )(got)
    side = flip(side, "c")
    send, gram = call(join_body, (shape(80, LANES), shape(16, LANES)), 3)(sums, side, gram)
    far = flip(send, "h")
    mix, basis = call(
        factor_body, (shape(32, LANES), shape(32, LANES)), 2, 500_000_000, 10_000_000
    )(gram, stack)
    send = call(combine_body, shape(OWNERS, 40, LANES), 4)(sums, side, far, mix)
    got = lax.all_to_all(send, FIRST + SECOND, 0, 0)
    hbm = pl.BlockSpec(memory_space=pltpu.HBM)
    corrected, factors = pl.pallas_call(
        update_body,
        out_shape=(shape(rows, cols, dtype=BF16), shape(2, RANK, cols)),
        in_specs=[VMEM] * 3,
        out_specs=(hbm, hbm),
        scratch_shapes=[
            pltpu.VMEM((rows, cols), BF16),
            pltpu.VMEM((2, RANK, cols), F32),
            pltpu.SemaphoreType.DMA((8,)),
        ],
        compiler_params=pltpu.CompilerParams(vmem_limit_bytes=40 * 2**20),
    )(got, weight, basis)
    return corrected[None], factors[None]


def solution(mesh):
    inner = Mesh(mesh.devices.reshape(2, 4, 2, 4, 4, 2), ("h", "y", "c", "x", "w", "v"))
    placed = (P(("h", "y", "c"), ("x", "w", "v"), None), P(("h", "y", "c"), None, None, None))
    return jax.shard_map(
        shards, mesh=inner, in_specs=placed, out_specs=placed, check_vma=False
    )
```

```python
import functools

import jax
import jax.numpy as jnp
from jax import lax
from jax.experimental import pallas as pl
from jax.experimental.pallas import tpu as pltpu
from jax.sharding import Mesh
from jax.sharding import PartitionSpec as P

RANK = 16
LANES = 128
FIRST, FIRST_SIZE = ("v", "x"), 8
SECOND, SECOND_SIZE = ("w",), 4
TILES = 40 // FIRST_SIZE
REST = TILES - SECOND_SIZE
OWNERS = FIRST_SIZE * SECOND_SIZE
GROUP = 32
HIGHEST = lax.Precision.HIGHEST
F32 = jnp.float32
BF16 = jnp.bfloat16
VMEM = pl.BlockSpec(memory_space=pltpu.VMEM)


def call(body, out, ins, flops=1_000_000, data=1_000_000):
    return pl.pallas_call(
        body,
        out_shape=out,
        in_specs=[VMEM] * ins,
        out_specs=jax.tree.map(lambda _: VMEM, out),
        compiler_params=pltpu.CompilerParams(vmem_limit_bytes=40 * 2**20),
        cost_estimate=pl.CostEstimate(flops=flops, bytes_accessed=data, transcendentals=0),
    )


def shape(*dims, dtype=F32):
    return jax.ShapeDtypeStruct(dims, dtype)


def dot(a, b, precision=HIGHEST):
    return jnp.dot(a, b, precision=precision, preferred_element_type=F32)


def dot_t(a, b, precision=HIGHEST):
    return lax.dot_general(
        a, b, (((1,), (1,)), ((), ())), precision=precision, preferred_element_type=F32
    )


def pieces(value):
    high = value.astype(BF16)
    return high, (value - high.astype(F32)).astype(BF16)


def signs():
    even = (1 - 2 * lax.axis_index("c")).astype(F32)
    low = (1 - 2 * lax.axis_index("h")).astype(F32)
    return even, low


def sketch_body(sketch_ref, starts_ref, weight_ref, send_ref):
    send_ref[0:16, :] = sketch_ref[0:16]
    send_ref[16:32, :] = dot_t(starts_ref[...].astype(BF16), weight_ref[...], None)


def differ_body(sketch_ref, mine_ref, side_ref, send_ref):
    even, _ = signs()
    send_ref[0:16, :] = even * (mine_ref[0:16] - side_ref[0:16])
    send_ref[16:32, :] = even * (sketch_ref[16:32] - side_ref[16:32])
    send_ref[32:48, :] = sketch_ref[16:32]


def project_body(mine_ref, far_ref, weight_ref, send_ref, stack_ref):
    _, low = signs()
    own, start_own = mine_ref[0:16], mine_ref[16:32]
    other, start_other = far_ref[0:16], far_ref[16:32]
    cross = low * (mine_ref[32:48] - far_ref[32:48])
    stack = jnp.concatenate([cross, own, other], axis=0)
    stack_ref[...] = stack
    zero = jnp.zeros((RANK, LANES), F32)

    def gram_rows(left, right):
        return dot_t(left, jnp.concatenate(right, axis=0))

    gram = (
        gram_rows(cross, [cross, own, other] + [zero] * 5)
        + gram_rows(own, [zero] * 3 + [own, other, start_own] + [zero] * 2)
        + gram_rows(other, [zero] * 6 + [other, start_other])
    )
    high, low_part = pieces(stack)
    both = jnp.concatenate([high, low_part], axis=0)
    for x in range(FIRST_SIZE):
        span = TILES * LANES
        product = jnp.dot(
            both, weight_ref[:, x * span : (x + 1) * span], preferred_element_type=F32
        )
        product = product[0:48] + product[48:96]
        for t in range(TILES):
            send_ref[x, t * 48 : (t + 1) * 48, :] = product[:, t * LANES : (t + 1) * LANES]
        send_ref[x, TILES * 48 : TILES * 48 + 16, :] = gram


def lane_group():
    return lax.broadcasted_iota(jnp.int32, (RANK, LANES), 1) // GROUP


def added(values):
    while len(values) > 1:
        values = [a + b for a, b in zip(values[::2], values[1::2])]
    return values[0]


def first_sum_body(got_ref, send_ref):
    def total(start, size):
        return added([got_ref[x, start : start + size, :] for x in range(FIRST_SIZE)])

    gram = total(TILES * 48, 16)
    lanes = lane_group()
    rests = [total((SECOND_SIZE + k) * 48, 48) for k in range(REST)]
    for z in range(SECOND_SIZE):
        send_ref[z, 0:48, :] = total(z * 48, 48)
        k, g = z // 4, z % 4
        packed = jnp.zeros((RANK, LANES), F32)
        for a in range(3):
            piece = rests[k][16 * a : 16 * a + 16]
            shift = (GROUP * (a - g)) % LANES
            if shift:
                piece = pltpu.roll(piece, shift, 1)
            packed = jnp.where(lanes == a, piece, packed)
        send_ref[z, 48:64, :] = packed
        send_ref[z, 64:80, :] = gram


def second_sum_body(got_ref, sums_ref, side_ref, gram_ref):
    total = added([got_ref[z] for z in range(SECOND_SIZE)])
    sums_ref[...] = total[0:64]
    side_ref[0:16, :] = total[16:32]
    side_ref[16:32, :] = total[48:64]
    gram_ref[...] = total[64:80]


def join_body(sums_ref, side_ref, gram_in_ref, send_ref, gram_ref):
    moved = pltpu.roll(side_ref[16:32], 2 * GROUP, 1)
    send_ref[0:48, :] = sums_ref[0:48]
    send_ref[48:64, :] = jnp.where(lane_group() == 3, moved, sums_ref[48:64])
    send_ref[64:80, :] = side_ref[0:16]
    gram_ref[...] = gram_in_ref[...]


def eye():
    rows = lax.broadcasted_iota(jnp.int32, (RANK, RANK), 0)
    cols = lax.broadcasted_iota(jnp.int32, (RANK, RANK), 1)
    return rows, (rows == cols).astype(F32)


def inverse_factors(grams):
    rows, unit = eye()
    left = list(grams)
    right = [unit] * len(grams)
    for j in range(RANK - 1):
        for i in range(len(grams)):
            ratio = left[i][:, j : j + 1] / left[i][j : j + 1, j : j + 1]
            ratio = jnp.where(rows > j, ratio, 0.0)
            left[i] = left[i] - ratio * left[i][j : j + 1, :]
            right[i] = right[i] - ratio * right[i][j : j + 1, :]
    out = []
    for i in range(len(grams)):
        pivots = jnp.sum(left[i] * unit, axis=1, keepdims=True)
        out.append(right[i] * lax.rsqrt(pivots))
    return out


def factor_body(gram_ref, stack_ref, mix_ref, basis_ref):
    even, low = signs()
    scale = -0.5 * low * even
    blocks = [gram_ref[:, 16 * b : 16 * b + 16] for b in range(8)]
    b0, b1, b2, b3, b4, b5, b6, b7 = blocks
    inv_own, inv_other = inverse_factors([b3, b6])
    gamma_own = dot(inv_own.T, inv_own)
    gamma_other = dot(inv_other.T, inv_other)
    q_own, q_other = b5.T, b7.T
    m_own = scale * dot(q_own, gamma_own)
    m_other = -scale * dot(q_other, gamma_other)
    kg0 = b0 + dot_t(m_own, b1) + dot_t(m_other, b2)
    kg1 = b1 + scale * q_own + dot_t(m_other, b4)
    kg2 = b2 + dot(m_own, b4) - scale * q_other
    gram1 = kg0 + dot_t(kg1, m_own) + dot_t(kg2, m_other)
    (inv1,) = inverse_factors([gram1])
    c_own = scale * even * dot(inv1, dot(kg1, gamma_own))
    c_other = -scale * even * dot(inv1, dot(kg2, gamma_other))
    n_own = dot(inv1, m_own)
    n_other = dot(inv1, m_other)
    zero = jnp.zeros((RANK, RANK), F32)
    first = [zero, even * inv_own, zero, -even * inv_own, zero, zero, zero, zero]
    second = [
        low * inv1,
        low * n_own + c_own,
        low * n_other,
        -c_own,
        -low * inv1,
        c_other - low * n_other,
        -low * n_own,
        -c_other,
    ]
    for b in range(8):
        mix_ref[0:16, 16 * b : 16 * b + 16] = first[b]
        mix_ref[16:32, 16 * b : 16 * b + 16] = second[b]
    cross, own, other = stack_ref[0:16], stack_ref[16:32], stack_ref[32:48]
    basis0 = (0.5 * even) * dot(inv_own, own)
    basis1 = (0.5 * low) * (dot(inv1, cross) + dot(n_own, own) + dot(n_other, other))
    basis_ref[...] = jnp.concatenate([basis0, basis1], axis=0)


def combine_body(sums_ref, side_ref, far_ref, mix_ref, send_ref):
    rest, far_rest = sums_ref[48:64], far_ref[48:64]

    def turned(value, a):
        return pltpu.roll(value, LANES - GROUP * a, 1) if a else value

    main = jnp.concatenate(
        [sums_ref[0:48], side_ref[0:16], far_ref[0:48], far_ref[64:80]], axis=0
    )
    tail = jnp.concatenate(
        [turned(rest, a) for a in range(3)]
        + [turned(side_ref[16:32], 1)]
        + [turned(far_rest, a) for a in range(4)],
        axis=0,
    )
    mix = mix_ref[...]
    head = dot(mix, main)
    tail = dot(mix, tail)
    lanes = lane_group()[0:8]
    packed = tail[0:8]
    for a in range(1, 4):
        packed = jnp.where(lanes == a, pltpu.roll(tail[8 * a : 8 * a + 8], GROUP * a, 1), packed)
    for n in range(send_ref.shape[0]):
        send_ref[n, 0:32, :] = head
        send_ref[n, 32:40, :] = packed


def update_body(
    got_ref, weight_ref, basis_ref, corrected_hbm, factors_hbm, corrected_ref, factors_ref, sems
):
    lanes = lane_group()[0:8]
    chunk = 10
    span = chunk * LANES
    transposed = basis_ref[...].T
    left = []
    for k in range(2):
        high, low = pieces(transposed[:, 16 * k : 16 * k + 16])
        left.append(jnp.concatenate([high, low, high], axis=1))
    copies = []
    for x in range(4):
        tiles = []
        for first in range(x * FIRST_SIZE // 4, (x + 1) * FIRST_SIZE // 4):
            base = first * SECOND_SIZE
            tiles += [got_ref[base + z, 0:32, :] for z in range(SECOND_SIZE)]
            for k in range(REST):
                groups = []
                for a in range(4):
                    row = None
                    for g in range(4):
                        piece = got_ref[base + 4 * k + g, 32:40, :]
                        shift = (GROUP * (g - a)) % LANES
                        if shift:
                            piece = pltpu.roll(piece, shift, 1)
                        row = piece if row is None else jnp.where(lanes == g, piece, row)
                    groups.append(row)
                tiles.append(jnp.concatenate(groups, axis=0))
        for t in range(0, chunk, 2):
            part = pl.ds(x * span + t * LANES, 2 * LANES)
            pair = jnp.concatenate(tiles[t : t + 2], axis=1)
            current = weight_ref[:, part].astype(F32)
            for k in range(2):
                factor = pair[16 * k : 16 * k + 16]
                factors_ref[k, :, part] = factor
                high, low = pieces(factor)
                right = jnp.concatenate([high, high, low], axis=0)
                change = jnp.dot(left[k], right, preferred_element_type=F32)
                rounded = (current - change).astype(BF16)
                current = rounded.astype(F32)
            corrected_ref[:, part] = rounded
            if t % 4 == 0 and t < 8:
                continue
            first, size = (x * span + (t - 2) * LANES, 4) if t < 8 else (x * span + t * LANES, 2)
            part = pl.ds(first, size * LANES)
            for i, (source, target) in enumerate(
                ((corrected_ref, corrected_hbm), (factors_ref, factors_hbm))
            ):
                index = (slice(None),) * (1 + i) + (part,)
                sem = sems.at[len(copies)]
                copy = pltpu.make_async_copy(source.at[index], target.at[index], sem)
                copy.start()
                copies.append(copy)
    for copy in copies:
        copy.wait()


def flip(value, axis):
    return lax.ppermute(value, axis, [(0, 1), (1, 0)])


def shards(weights, warm_start):
    weight = weights[0]
    starts = warm_start[0]
    rows, cols = weight.shape
    swapped = flip(starts[1].astype(F32), "c")
    sketch = lax.dot_general(
        starts.reshape(2 * RANK, cols),
        weight,
        (((1,), (1,)), ((), ())),
        preferred_element_type=F32,
    )
    mine = call(sketch_body, shape(32, rows), 3)(sketch, swapped, weight)
    mine = call(differ_body, shape(48, rows), 3)(sketch, mine, flip(mine, "c"))
    far = flip(mine, "h")
    depth = TILES * 48 + 16
    send, stack = call(
        project_body, (shape(FIRST_SIZE, depth, LANES), shape(48, LANES)), 3, 130_000_000, 4_000_000
    )(mine, far, weight)
    got = lax.all_to_all(send, FIRST, 0, 0)
    send = call(first_sum_body, shape(SECOND_SIZE, 80, LANES), 1)(got)
    got = lax.all_to_all(send, SECOND, 0, 0)
    sums, side, gram = call(
        second_sum_body, (shape(64, LANES), shape(32, LANES), shape(16, LANES)), 1
    )(got)
    side = flip(side, "c")
    send, gram = call(join_body, (shape(80, LANES), shape(16, LANES)), 3)(sums, side, gram)
    far = flip(send, "h")
    mix, basis = call(
        factor_body, (shape(32, LANES), shape(32, LANES)), 2, 500_000_000, 10_000_000
    )(gram, stack)
    send = call(combine_body, shape(OWNERS, 40, LANES), 4)(sums, side, far, mix)
    got = lax.all_to_all(send, FIRST + SECOND, 0, 0)
    hbm = pl.BlockSpec(memory_space=pltpu.HBM)
    corrected, factors = pl.pallas_call(
        update_body,
        out_shape=(shape(rows, cols, dtype=BF16), shape(2, RANK, cols)),
        in_specs=[VMEM] * 3,
        out_specs=(hbm, hbm),
        scratch_shapes=[
            pltpu.VMEM((rows, cols), BF16),
            pltpu.VMEM((2, RANK, cols), F32),
            pltpu.SemaphoreType.DMA((24,)),
        ],
        compiler_params=pltpu.CompilerParams(vmem_limit_bytes=40 * 2**20),
    )(got, weight, basis)
    return corrected[None], factors[None]


def solution(mesh):
    inner = Mesh(mesh.devices.reshape(2, 4, 2, 4, 4, 2), ("h", "y", "c", "x", "w", "v"))
    placed = (P(("h", "y", "c"), ("x", "w", "v"), None), P(("h", "y", "c"), None, None, None))
    return jax.shard_map(
        shards, mesh=inner, in_specs=placed, out_specs=placed, check_vma=False
    )
```

```python
import functools

import jax
import jax.numpy as jnp
from jax import lax
from jax.experimental import pallas as pl
from jax.experimental.pallas import tpu as pltpu
from jax.sharding import Mesh
from jax.sharding import PartitionSpec as P

RANK = 16
LANES = 128
FIRST, FIRST_SIZE = ("v", "x"), 8
SECOND, SECOND_SIZE = ("w",), 4
TILES = 40 // FIRST_SIZE
REST = TILES - SECOND_SIZE
OWNERS = FIRST_SIZE * SECOND_SIZE
GROUP = 32
HIGHEST = lax.Precision.HIGHEST
F32 = jnp.float32
BF16 = jnp.bfloat16
VMEM = pl.BlockSpec(memory_space=pltpu.VMEM)


def call(body, out, ins, flops=1_000_000, data=1_000_000):
    return pl.pallas_call(
        body,
        out_shape=out,
        in_specs=[VMEM] * ins,
        out_specs=jax.tree.map(lambda _: VMEM, out),
        compiler_params=pltpu.CompilerParams(vmem_limit_bytes=40 * 2**20),
        cost_estimate=pl.CostEstimate(flops=flops, bytes_accessed=data, transcendentals=0),
    )


def shape(*dims, dtype=F32):
    return jax.ShapeDtypeStruct(dims, dtype)


def dot(a, b, precision=HIGHEST):
    return jnp.dot(a, b, precision=precision, preferred_element_type=F32)


def dot_t(a, b, precision=HIGHEST):
    return lax.dot_general(
        a, b, (((1,), (1,)), ((), ())), precision=precision, preferred_element_type=F32
    )


def pieces(value):
    high = value.astype(BF16)
    return high, (value - high.astype(F32)).astype(BF16)


def signs():
    even = (1 - 2 * lax.axis_index("c")).astype(F32)
    low = (1 - 2 * lax.axis_index("h")).astype(F32)
    return even, low


def sketch_body(sketch_ref, starts_ref, weight_ref, send_ref):
    send_ref[0:16, :] = sketch_ref[0:16]
    send_ref[16:32, :] = dot_t(starts_ref[...].astype(BF16), weight_ref[...], None)


def differ_body(sketch_ref, mine_ref, side_ref, send_ref):
    even, _ = signs()
    send_ref[0:16, :] = even * (mine_ref[0:16] - side_ref[0:16])
    send_ref[16:32, :] = even * (sketch_ref[16:32] - side_ref[16:32])
    send_ref[32:48, :] = sketch_ref[16:32]


def project_body(mine_ref, far_ref, weight_ref, send_ref, stack_ref):
    _, low = signs()
    own, start_own = mine_ref[0:16], mine_ref[16:32]
    other, start_other = far_ref[0:16], far_ref[16:32]
    cross = low * (mine_ref[32:48] - far_ref[32:48])
    stack = jnp.concatenate([cross, own, other], axis=0)
    stack_ref[...] = stack
    zero = jnp.zeros((RANK, LANES), F32)

    def gram_rows(left, right):
        return dot_t(left, jnp.concatenate(right, axis=0))

    gram = (
        gram_rows(cross, [cross, own, other] + [zero] * 5)
        + gram_rows(own, [zero] * 3 + [own, other, start_own] + [zero] * 2)
        + gram_rows(other, [zero] * 6 + [other, start_other])
    )
    high, low_part = pieces(stack)
    both = jnp.concatenate([high, low_part], axis=0)
    for x in range(FIRST_SIZE):
        span = TILES * LANES
        product = jnp.dot(
            both, weight_ref[:, x * span : (x + 1) * span], preferred_element_type=F32
        )
        product = product[0:48] + product[48:96]
        for t in range(TILES):
            send_ref[x, t * 48 : (t + 1) * 48, :] = product[:, t * LANES : (t + 1) * LANES]
        send_ref[x, TILES * 48 : TILES * 48 + 16, :] = gram


def lane_group():
    return lax.broadcasted_iota(jnp.int32, (RANK, LANES), 1) // GROUP


def added(values):
    while len(values) > 1:
        values = [a + b for a, b in zip(values[::2], values[1::2])]
    return values[0]


def first_sum_body(got_ref, send_ref):
    def total(start, size):
        return added([got_ref[x, start : start + size, :] for x in range(FIRST_SIZE)])

    gram = total(TILES * 48, 16)
    lanes = lane_group()
    rests = [total((SECOND_SIZE + k) * 48, 48) for k in range(REST)]
    for z in range(SECOND_SIZE):
        send_ref[z, 0:48, :] = total(z * 48, 48)
        k, g = z // 4, z % 4
        packed = jnp.zeros((RANK, LANES), F32)
        for a in range(3):
            piece = rests[k][16 * a : 16 * a + 16]
            shift = (GROUP * (a - g)) % LANES
            if shift:
                piece = pltpu.roll(piece, shift, 1)
            packed = jnp.where(lanes == a, piece, packed)
        send_ref[z, 48:64, :] = packed
        send_ref[z, 64:80, :] = gram


def second_sum_body(got_ref, sums_ref, side_ref, gram_ref):
    total = added([got_ref[z] for z in range(SECOND_SIZE)])
    sums_ref[...] = total[0:64]
    side_ref[0:16, :] = total[16:32]
    side_ref[16:32, :] = total[48:64]
    gram_ref[...] = total[64:80]


def join_body(sums_ref, side_ref, gram_in_ref, send_ref, gram_ref):
    moved = pltpu.roll(side_ref[16:32], 2 * GROUP, 1)
    send_ref[0:48, :] = sums_ref[0:48]
    send_ref[48:64, :] = jnp.where(lane_group() == 3, moved, sums_ref[48:64])
    send_ref[64:80, :] = side_ref[0:16]
    gram_ref[...] = gram_in_ref[...]


def eye():
    rows = lax.broadcasted_iota(jnp.int32, (RANK, RANK), 0)
    cols = lax.broadcasted_iota(jnp.int32, (RANK, RANK), 1)
    return rows, (rows == cols).astype(F32)


def inverse_factors(grams):
    rows, unit = eye()
    left = list(grams)
    right = [unit] * len(grams)
    for j in range(RANK - 1):
        for i in range(len(grams)):
            ratio = left[i][:, j : j + 1] / left[i][j : j + 1, j : j + 1]
            ratio = jnp.where(rows > j, ratio, 0.0)
            left[i] = left[i] - ratio * left[i][j : j + 1, :]
            right[i] = right[i] - ratio * right[i][j : j + 1, :]
    out = []
    for i in range(len(grams)):
        pivots = jnp.sum(left[i] * unit, axis=1, keepdims=True)
        out.append(right[i] * lax.rsqrt(pivots))
    return out


def factor_body(gram_ref, stack_ref, mix_ref, basis_ref):
    even, low = signs()
    scale = -0.5 * low * even
    blocks = [gram_ref[:, 16 * b : 16 * b + 16] for b in range(8)]
    b0, b1, b2, b3, b4, b5, b6, b7 = blocks
    inv_own, inv_other = inverse_factors([b3, b6])
    gamma_own = dot(inv_own.T, inv_own)
    gamma_other = dot(inv_other.T, inv_other)
    q_own, q_other = b5.T, b7.T
    m_own = scale * dot(q_own, gamma_own)
    m_other = -scale * dot(q_other, gamma_other)
    kg0 = b0 + dot_t(m_own, b1) + dot_t(m_other, b2)
    kg1 = b1 + scale * q_own + dot_t(m_other, b4)
    kg2 = b2 + dot(m_own, b4) - scale * q_other
    gram1 = kg0 + dot_t(kg1, m_own) + dot_t(kg2, m_other)
    (inv1,) = inverse_factors([gram1])
    c_own = scale * even * dot(inv1, dot(kg1, gamma_own))
    c_other = -scale * even * dot(inv1, dot(kg2, gamma_other))
    n_own = dot(inv1, m_own)
    n_other = dot(inv1, m_other)
    zero = jnp.zeros((RANK, RANK), F32)
    first = [zero, even * inv_own, zero, -even * inv_own, zero, zero, zero, zero]
    second = [
        low * inv1,
        low * n_own + c_own,
        low * n_other,
        -c_own,
        -low * inv1,
        c_other - low * n_other,
        -low * n_own,
        -c_other,
    ]
    for b in range(8):
        mix_ref[0:16, 16 * b : 16 * b + 16] = first[b]
        mix_ref[16:32, 16 * b : 16 * b + 16] = second[b]
    cross, own, other = stack_ref[0:16], stack_ref[16:32], stack_ref[32:48]
    basis0 = (0.5 * even) * dot(inv_own, own)
    basis1 = (0.5 * low) * (dot(inv1, cross) + dot(n_own, own) + dot(n_other, other))
    basis_ref[...] = jnp.concatenate([basis0, basis1], axis=0)


def combine_body(sums_ref, side_ref, far_ref, mix_ref, send_ref):
    rest, far_rest = sums_ref[48:64], far_ref[48:64]

    def turned(value, a):
        return pltpu.roll(value, LANES - GROUP * a, 1) if a else value

    main = jnp.concatenate(
        [sums_ref[0:48], side_ref[0:16], far_ref[0:48], far_ref[64:80]], axis=0
    )
    tail = jnp.concatenate(
        [turned(rest, a) for a in range(3)]
        + [turned(side_ref[16:32], 1)]
        + [turned(far_rest, a) for a in range(4)],
        axis=0,
    )
    mix = mix_ref[...]
    head = dot(mix, main)
    tail = dot(mix, tail)
    lanes = lane_group()[0:8]
    packed = tail[0:8]
    for a in range(1, 4):
        packed = jnp.where(lanes == a, pltpu.roll(tail[8 * a : 8 * a + 8], GROUP * a, 1), packed)
    for n in range(send_ref.shape[0]):
        send_ref[n, 0:32, :] = head
        send_ref[n, 32:40, :] = packed


def update_body(
    got_ref, weight_ref, basis_ref, corrected_hbm, factors_hbm, corrected_ref, factors_ref, sems
):
    lanes = lane_group()[0:8]
    chunk = 10
    span = chunk * LANES
    transposed = basis_ref[...].T
    left = []
    for k in range(2):
        high, low = pieces(transposed[:, 16 * k : 16 * k + 16])
        left.append(jnp.concatenate([high, low, high], axis=1))
    copies = []
    for x in range(4):
        tiles = []
        for first in range(x * FIRST_SIZE // 4, (x + 1) * FIRST_SIZE // 4):
            v, x_index = first // 4, first % 4
            owners = [v * 16 + w * 4 + x_index for w in range(SECOND_SIZE)]
            tiles += [got_ref[owner, 0:32, :] for owner in owners]
            for k in range(REST):
                groups = []
                for a in range(4):
                    row = None
                    for g in range(4):
                        piece = got_ref[owners[4 * k + g], 32:40, :]
                        shift = (GROUP * (g - a)) % LANES
                        if shift:
                            piece = pltpu.roll(piece, shift, 1)
                        row = piece if row is None else jnp.where(lanes == g, piece, row)
                    groups.append(row)
                tiles.append(jnp.concatenate(groups, axis=0))
        for t in range(0, chunk, 2):
            part = pl.ds(x * span + t * LANES, 2 * LANES)
            pair = jnp.concatenate(tiles[t : t + 2], axis=1)
            current = weight_ref[:, part].astype(F32)
            for k in range(2):
                factor = pair[16 * k : 16 * k + 16]
                factors_ref[k, :, part] = factor
                high, low = pieces(factor)
                right = jnp.concatenate([high, high, low], axis=0)
                change = jnp.dot(left[k], right, preferred_element_type=F32)
                rounded = (current - change).astype(BF16)
                current = rounded.astype(F32)
            corrected_ref[:, part] = rounded
            if t % 4 == 0 and t < 8:
                continue
            first, size = (x * span + (t - 2) * LANES, 4) if t < 8 else (x * span + t * LANES, 2)
            part = pl.ds(first, size * LANES)
            for i, (source, target) in enumerate(
                ((corrected_ref, corrected_hbm), (factors_ref, factors_hbm))
            ):
                index = (slice(None),) * (1 + i) + (part,)
                sem = sems.at[len(copies)]
                copy = pltpu.make_async_copy(source.at[index], target.at[index], sem)
                copy.start()
                copies.append(copy)
    for copy in copies:
        copy.wait()


def flip(value, axis):
    return lax.ppermute(value, axis, [(0, 1), (1, 0)])


def shards(weights, warm_start):
    weight = weights[0]
    starts = warm_start[0]
    rows, cols = weight.shape
    swapped = flip(starts[1].astype(F32), "c")
    sketch = lax.dot_general(
        starts.reshape(2 * RANK, cols),
        weight,
        (((1,), (1,)), ((), ())),
        preferred_element_type=F32,
    )
    mine = call(sketch_body, shape(32, rows), 3)(sketch, swapped, weight)
    mine = call(differ_body, shape(48, rows), 3)(sketch, mine, flip(mine, "c"))
    far = flip(mine, "h")
    depth = TILES * 48 + 16
    send, stack = call(
        project_body, (shape(FIRST_SIZE, depth, LANES), shape(48, LANES)), 3, 130_000_000, 4_000_000
    )(mine, far, weight)
    got = lax.all_to_all(send, FIRST, 0, 0)
    send = call(first_sum_body, shape(SECOND_SIZE, 80, LANES), 1)(got)
    got = lax.all_to_all(send, SECOND, 0, 0)
    sums, side, gram = call(
        second_sum_body, (shape(64, LANES), shape(32, LANES), shape(16, LANES)), 1
    )(got)
    side = flip(side, "c")
    send, gram = call(join_body, (shape(80, LANES), shape(16, LANES)), 3)(sums, side, gram)
    far = flip(send, "h")
    mix, basis = call(
        factor_body, (shape(32, LANES), shape(32, LANES)), 2, 500_000_000, 10_000_000
    )(gram, stack)
    send = call(combine_body, shape(OWNERS, 40, LANES), 4)(sums, side, far, mix)
    got = lax.all_to_all(send, ("v", "w", "x"), 0, 0)
    hbm = pl.BlockSpec(memory_space=pltpu.HBM)
    corrected, factors = pl.pallas_call(
        update_body,
        out_shape=(shape(rows, cols, dtype=BF16), shape(2, RANK, cols)),
        in_specs=[VMEM] * 3,
        out_specs=(hbm, hbm),
        scratch_shapes=[
            pltpu.VMEM((rows, cols), BF16),
            pltpu.VMEM((2, RANK, cols), F32),
            pltpu.SemaphoreType.DMA((24,)),
        ],
        compiler_params=pltpu.CompilerParams(vmem_limit_bytes=40 * 2**20),
    )(got, weight, basis)
    return corrected[None], factors[None]


def solution(mesh):
    inner = Mesh(mesh.devices.reshape(2, 4, 2, 4, 4, 2), ("h", "y", "c", "x", "w", "v"))
    placed = (P(("h", "y", "c"), ("x", "w", "v"), None), P(("h", "y", "c"), None, None, None))
    return jax.shard_map(
        shards, mesh=inner, in_specs=placed, out_specs=placed, check_vma=False
    )
```
